32 devices in a mesh: grp: 2 (over y), sec: 8 (over z, core), mpo: 2 (over x), sub: 1.
Axes of the slice: x: 2, y: 2, z: 4, core: 2. Of those that a mesh axis runs over, the one named last changes fastest.
Arguments:
- psi: bfloat16 [48, 512, 512], P(('grp', 'sec')), parts along dimension 0, may hold values from -6 to 6
- left_env: bfloat16 [14, 48, 512, 512], P('mpo', ('grp', 'sec')), parts along dimension 1, may hold values from -0.0625 to 0.0625
- right_env: bfloat16 [14, 48, 512, 512], P('mpo', ('grp', 'sec'), None, 'sub'), parts along dimension 1, may hold values from -0.25 to 0.25
- targets: int32 [24, 14], P('sec', 'mpo'), may hold values from 0 to 23, as said below
Outputs:
- sigma: bfloat16 [48, 512, 512], P(('grp', 'sec'), None, 'sub'), parts along dimension 0
The draws below stay inside these ranges and needn't reach their ends.
There are 2 independent parts, one for each index of `grp`. The reference program is written for one: setup_inputs(seed, part) draws one part's arguments, and reference() takes and returns one part's arrays. A program takes and returns all parts, laid end to end along the dimension named above; an argument that names none is the same for every part. Nothing has to cross between parts.
Inputs may be any that keep to these rules, and one draw needn't show every extreme that they name: Among the entries of one device's block (one index of sec and one of mpo, 3 x 7 entries), at most 3 have targets // 3 equal to any one index of sec, and exactly 3 for some index.
All inputs are finite; a program needn't handle non-finite values.
Results may differ from the reference program's by a relative error of at most 0.0058.
Values may be sent and summed in bfloat16 or wider, within the bound.
A program may use at most 128 MiB of HBM per device.

```python
import jax
import jax.numpy as jnp
from jax import lax

S = 512
SEC_DEV = 3
W_DEV = 7
P_SIZE = 24
W = 14
CAP = 3


def draw_targets(key, part):
    key = jax.random.fold_in(key, 7)
    sec_count = P_SIZE // SEC_DEV
    mpo_count = W // W_DEV
    row_count = SEC_DEV * W_DEV
    block_keys = jax.random.split(key, sec_count * mpo_count)

    def one_block(block_key):
        first_key, second_key, third_key, fourth_key = jax.random.split(block_key, 4)
        crowded = jax.random.randint(first_key, (), 0, sec_count).astype(jnp.int32)
        others = jax.random.permutation(second_key, (sec_count - 1) * CAP)[:row_count - CAP] // CAP
        others = others.astype(jnp.int32)
        others = others + (others >= crowded).astype(jnp.int32)
        owners = jnp.concatenate([jnp.full((CAP,), 1, jnp.int32) * crowded, others])
        owners = jax.random.permutation(third_key, owners)
        within = jax.random.randint(fourth_key, (row_count,), 0, SEC_DEV).astype(jnp.int32)
        return (owners * SEC_DEV + within).reshape(SEC_DEV, W_DEV)
    blocks = jax.vmap(one_block)(block_keys).reshape(sec_count, mpo_count, SEC_DEV, W_DEV)
    return blocks.transpose(0, 2, 1, 3).reshape(P_SIZE, W).astype(jnp.int32)


def block_levels(own_key, extent, shards, smallest, top_value):
    def one(position, parts):
        draws = jax.random.uniform(jax.random.fold_in(jax.random.fold_in(own_key, 6), position), (parts,), jnp.float32, smallest / len(shards), top_value / len(shards))
        return jnp.repeat(jnp.exp(draws), extent[position] // parts).reshape((-1,) + (1,) * (len(extent) - position - 1))

    level = one(*shards[0])
    for cut in shards[1:]:
        level = level * one(*cut)
    return level


def centred(rng, extent, width, limit, cuts=(), held_as=jnp.bfloat16):
    values = width * jax.random.normal(rng, extent, jnp.float32)
    if cuts:
        values = values * block_levels(rng, extent, cuts, -0.22, 0.18)
    return jnp.clip(values, -limit, limit).astype(held_as)


def setup_inputs(seed: int = 0, part: int = 0) -> dict:
    key_list = jax.random.split(jax.random.key(seed), 5)
    own_keys = jax.random.split(jax.random.fold_in(key_list[4], part), 5)
    return {
        "psi": centred(own_keys[0], (P_SIZE, S, S), 1.0, 6.0, ((0, 8),)),
        "left_env": centred(own_keys[1], (W, P_SIZE, S, S), (S * W) ** -0.5, 0.0625, ((0, 2), (1, 8))),
        "right_env": centred(own_keys[2], (W, P_SIZE, S, S), S ** -0.5, 0.25, ((0, 2), (1, 8))),
        "targets": draw_targets(jax.random.fold_in(key_list[4], 71), part),
    }


def reference(psi, left_env, right_env, targets):
    def one_source(index, sigma):
        block = lax.dynamic_index_in_dim(psi, index, 0, False)
        rights = lax.dynamic_index_in_dim(right_env, index, 1, False)
        lefts = lax.dynamic_index_in_dim(left_env, index, 1, False)
        inner = jnp.einsum("ab,wbc->wac", block.astype(jnp.float32), rights.astype(jnp.float32)).astype(jnp.bfloat16)
        contrib = jnp.einsum("wab,wbc->wac", lefts.astype(jnp.float32), inner.astype(jnp.float32)).astype(jnp.bfloat16)
        where_to = lax.dynamic_index_in_dim(targets, index, 0, False).astype(jnp.int32)
        return sigma.at[where_to].add(contrib.astype(jnp.float32))

    start = jnp.zeros((P_SIZE, S, S), jnp.float32)
    sigma = lax.fori_loop(0, P_SIZE, one_source, start)
    return sigma.astype(jnp.bfloat16)
```

```python
import jax
import jax.numpy as jnp
from jax import lax
from jax.sharding import PartitionSpec as P


def local(psi, left_env, right_env, targets):
    sec_count = lax.axis_size("sec")
    sec_dev = psi.shape[0]
    width = psi.shape[1]
    terms_dev = left_env.shape[0]
    row_count = sec_dev * terms_dev
    inner = jnp.einsum("jab,wjbc->wjac", psi, right_env, preferred_element_type=jnp.float32).astype(
        jnp.bfloat16
    )
    contrib = jnp.einsum(
        "wjab,wjbc->jwac", left_env, inner, preferred_element_type=jnp.float32
    ).astype(jnp.bfloat16)
    half_width = contrib.shape[-1]
    contrib = contrib.reshape(row_count, width, half_width)
    flat_targets = targets.reshape(row_count)
    placing = (jnp.arange(sec_count * sec_dev)[:, None] == flat_targets[None, :]).astype(jnp.bfloat16)
    partial = jnp.einsum(
        "kr,rac->kac", placing, contrib, preferred_element_type=jnp.float32
    ).astype(jnp.bfloat16)
    mine = lax.psum_scatter(partial, "sec", scatter_dimension=0, tiled=True)
    total = lax.psum(mine.astype(jnp.float32), "mpo")
    return total.astype(jnp.bfloat16)


def solution(mesh):
    placed = (
        P(("grp", "sec"), None, None),
        P("mpo", ("grp", "sec"), None, None),
        P("mpo", ("grp", "sec"), None, "sub"),
        P("sec", "mpo"),
    )
    return jax.shard_map(
        local, mesh=mesh, in_specs=placed, out_specs=P(("grp", "sec"), None, "sub"), check_vma=False
    )
```

```python
import functools

import jax
import jax.numpy as jnp
from jax import lax
from jax.experimental import pallas as pl
from jax.experimental.pallas import tpu as pltpu
from jax.sharding import PartitionSpec as P

MESH = pl.DeviceIdType.MESH
F32 = jnp.float32
BF16 = jnp.bfloat16


def first_rows(width, mpo):
    return max(16, (width * 2 // 3 // mpo + 8) // 16 * 16)


def kernel(
    n, cores, mpo, cap, hx,
    slots_ref, marks_ref, psi_hbm, left_hbm, right_hbm, out_ref,
    pv, lv, rv, sib_send, sib_recv, own_p, own_b, x_recv, z_p, z_b, fin_p, fin_b,
    in_sem, sib_ssem, sib_rsem, x_ssem, x_rsem, zp_ssem, zp_rsem, zb_ssem, zb_rsem,
    fp_ssem, fp_rsem, fb_ssem, fb_rsem,
):
    terms = lv.shape[0]
    sec_dev, width, cols = pv.shape[0], lv.shape[1], rv.shape[2]
    hb = width - mpo * hx
    sec = lax.axis_index("sec")
    me = lax.axis_index("mpo")
    z = lax.div(sec, cores)
    c = lax.rem(sec, cores)
    sibling = {"sec": z * cores + (1 - c)}
    right_dev = {"sec": sec + cores}
    left_dev = {"sec": sec - cores}

    def other(d):
        return lax.rem(me + d, mpo)

    def load_psi():
        return pltpu.make_async_copy(psi_hbm, pv, in_sem.at[2 * terms])

    def load_right(r):
        return pltpu.make_async_copy(right_hbm.at[r], rv.at[r], in_sem.at[r])

    def load_left(r):
        return pltpu.make_async_copy(left_hbm.at[r], lv.at[r], in_sem.at[terms + r])

    load_psi().start()

    @pl.loop(0, terms)
    def _(r):
        load_right(r).start()

    @pl.loop(0, terms)
    def _(r):
        load_left(r).start()

    barrier = pltpu.get_barrier_semaphore()
    if cores == 2:
        pl.semaphore_signal(barrier, inc=1, device_id=sibling, device_id_type=MESH)
    for d in range(1, mpo):
        pl.semaphore_signal(barrier, inc=1, device_id={"mpo": other(d)}, device_id_type=MESH)

    @pl.when(z > 0)
    def _():
        pl.semaphore_signal(barrier, inc=1, device_id=left_dev, device_id_type=MESH)

    @pl.when(z < n - 1)
    def _():
        pl.semaphore_signal(barrier, inc=1, device_id=right_dev, device_id_type=MESH)

    peers = cores - 1 + mpo - 1 + jnp.minimum(z, 1) + jnp.minimum(n - 1 - z, 1)
    pl.semaphore_wait(barrier, peers)

    def target(k):
        near_left = 2 * z <= n - 1
        lead = jnp.where(near_left, n - 1 - 2 * z, 2 * z - (n - 1))
        q = jnp.maximum(k - lead, 0)
        half = lax.div(q, 2)
        odd = lax.rem(q, 2) == 1
        ahead = jnp.minimum(k, lead)
        t_left = jnp.where(odd, half, n - 1 - ahead - half)
        t_right = jnp.where(odd, n - 1 - half, ahead + half)
        return jnp.where(near_left, t_left, t_right)

    def sib_copy(t):
        return pltpu.make_async_remote_copy(
            src_ref=sib_send.at[t], dst_ref=sib_recv.at[t],
            send_sem=sib_ssem.at[t], recv_sem=sib_rsem.at[t],
            device_id=sibling, device_id_type=MESH)

    def x_copy(t, s, d):
        return pltpu.make_async_remote_copy(
            src_ref=own_p.at[t, other(d), s], dst_ref=x_recv.at[mpo - d - 1, t, s],
            send_sem=x_ssem.at[d - 1, t, s], recv_sem=x_rsem.at[mpo - d - 1, t, s],
            device_id={"mpo": other(d)}, device_id_type=MESH)

    def x_wait(t, s, d):
        pltpu.make_async_remote_copy(
            src_ref=own_p.at[t, other(d), s], dst_ref=x_recv.at[d - 1, t, s],
            send_sem=x_ssem.at[d - 1, t, s], recv_sem=x_rsem.at[d - 1, t, s],
            device_id={"mpo": other(d)}, device_id_type=MESH).wait_recv()

    def zp_copy(t, s, slot, dev):
        return pltpu.make_async_remote_copy(
            src_ref=own_p.at[t, me, s], dst_ref=z_p.at[slot, s],
            send_sem=zp_ssem.at[t, s], recv_sem=zp_rsem.at[slot, s],
            device_id=dev, device_id_type=MESH)

    def zb_copy(t, s, slot, dev):
        return pltpu.make_async_remote_copy(
            src_ref=own_b.at[t, s], dst_ref=z_b.at[slot, s],
            send_sem=zb_ssem.at[t, s], recv_sem=zb_rsem.at[slot, s],
            device_id=dev, device_id_type=MESH)

    def z_send(copy, t, s):
        @pl.when(t > z)
        def _():
            copy(t, s, t, right_dev).start()

        @pl.when(t < z)
        def _():
            copy(t, s, jnp.where(t == z - 1, n, t), left_dev).start()

    def fp_copy(s, d):
        return pltpu.make_async_remote_copy(
            src_ref=fin_p.at[me, s], dst_ref=fin_p.at[me, s],
            send_sem=fp_ssem.at[d - 1, s], recv_sem=fp_rsem.at[me, s],
            device_id={"mpo": other(d)}, device_id_type=MESH)

    def fb_copy(s, d):
        return pltpu.make_async_remote_copy(
            src_ref=fin_b.at[me, s], dst_ref=fin_b.at[me, s],
            send_sem=fb_ssem.at[d - 1, s], recv_sem=fb_rsem.at[me, s],
            device_id={"mpo": other(d)}, device_id_type=MESH)

    def fp_wait(s, d):
        o = other(d)
        pltpu.make_async_remote_copy(
            src_ref=fin_p.at[o, s], dst_ref=fin_p.at[o, s],
            send_sem=fp_ssem.at[d - 1, s], recv_sem=fp_rsem.at[o, s],
            device_id={"mpo": o}, device_id_type=MESH).wait_recv()

    def fb_wait(s, d):
        o = other(d)
        pltpu.make_async_remote_copy(
            src_ref=fin_b.at[o, s], dst_ref=fin_b.at[o, s],
            send_sem=fb_ssem.at[d - 1, s], recv_sem=fb_rsem.at[o, s],
            device_id={"mpo": o}, device_id_type=MESH).wait_recv()

    load_psi().wait()
    col_tile = min(cols, 256)

    @pl.loop(0, terms)
    def _(r):
        load_right(r).wait()
        j = lax.rem(r, sec_dev)
        for c0 in range(0, cols, col_tile):
            rv[r, :, c0:c0 + col_tile] = jnp.dot(
                pv[j], rv[r, :, c0:c0 + col_tile], preferred_element_type=F32
            ).astype(BF16)

    @pl.loop(0, terms)
    def _(r):
        load_left(r).wait()

    def partial_rows(owner, row0, rows):
        products = []
        for i in range(cap):
            r = slots_ref[owner * cap + i]
            products.append(jnp.dot(lv[r, row0:row0 + rows, :], rv[r], preferred_element_type=F32))
        for s in range(sec_dev):
            total = None
            for i in range(cap):
                term = products[i] * marks_ref[(owner * cap + i) * sec_dev + s]
                total = term if total is None else total + term
            yield s, total.astype(BF16)

    parts = [(m * hx, hx, m) for m in range(mpo)] + [(mpo * hx, hb, None)]

    def make_sums(t):
        if cores == 2:
            for row0, rows, m in parts:
                for s, value in partial_rows(t * cores + (1 - c), row0, rows):
                    sib_send[t, s, row0:row0 + rows, :] = value
            sib_copy(t).start()
        for row0, rows, m in parts:
            for s, value in partial_rows(t * cores + c, row0, rows):
                if m is None:
                    own_b[t, s] = value
                else:
                    own_p[t, m, s] = value

    def add_sibling(t):
        if cores == 2:
            sib_copy(t).wait_recv()
        for s in range(sec_dev):
            if cores == 2:
                for m in range(mpo):
                    own_p[t, m, s] = (
                        own_p[t, m, s].astype(F32)
                        + sib_recv[t, s, m * hx:(m + 1) * hx, :].astype(F32)
                    ).astype(BF16)
                own_b[t, s] = (
                    own_b[t, s].astype(F32) + sib_recv[t, s, mpo * hx:, :].astype(F32)
                ).astype(BF16)
            for d in range(1, mpo):
                x_copy(t, s, d).start()

            @pl.when(z == 0)
            def _():
                @pl.when(t > 0)
                def _():
                    zb_copy(t, s, t, right_dev).start()

            @pl.when(z == n - 1)
            def _():
                @pl.when(t < n - 1)
                def _():
                    zb_copy(t, s, jnp.where(t == z - 1, n, t), left_dev).start()

    @pl.loop(0, n)
    def _(k):
        make_sums(target(k))

        @pl.when(k > 0)
        def _():
            add_sibling(target(k - 1))

    add_sibling(z)

    def add_to(ref, values):
        total = ref[...].astype(F32)
        for v in values:
            total = total + v.astype(F32)
        ref[...] = total.astype(BF16)

    @pl.loop(0, n - 1)
    def _(k):
        t = target(k)
        inside = jnp.logical_or(jnp.logical_and(t > z, z > 0), jnp.logical_and(t < z, z < n - 1))

        @pl.loop(0, sec_dev)
        def _(s):
            @pl.when(inside)
            def _():
                zb_copy(t, s, t, right_dev).wait_recv()
                add_to(own_b.at[t, s], [z_b[t, s]])
                z_send(zb_copy, t, s)

            for d in range(1, mpo):
                x_wait(t, s, d)

            @pl.when(inside)
            def _():
                zp_copy(t, s, t, right_dev).wait_recv()
                add_to(own_p.at[t, me, s], [x_recv[d, t, s] for d in range(mpo - 1)] + [z_p[t, s]])

            @pl.when(jnp.logical_not(inside))
            def _():
                add_to(own_p.at[t, me, s], [x_recv[d, t, s] for d in range(mpo - 1)])

            z_send(zp_copy, t, s)

    @pl.loop(0, sec_dev)
    def _(s):
        @pl.when(z > 0)
        def _():
            zb_copy(z, s, z, left_dev).wait_recv()
            add_to(own_b.at[z, s], [z_b[z, s]])

        @pl.when(z < n - 1)
        def _():
            zb_copy(z, s, n, right_dev).wait_recv()
            add_to(own_b.at[z, s], [z_b[n, s]])

        fin_b[me, s] = own_b[z, s]
        for d in range(1, mpo):
            fb_copy(s, d).start()
            x_wait(z, s, d)
        add_to(own_p.at[z, me, s], [x_recv[d, z, s] for d in range(mpo - 1)])

        @pl.when(z > 0)
        def _():
            zp_copy(z, s, z, left_dev).wait_recv()
            add_to(own_p.at[z, me, s], [z_p[z, s]])

        @pl.when(z < n - 1)
        def _():
            zp_copy(z, s, n, right_dev).wait_recv()
            add_to(own_p.at[z, me, s], [z_p[n, s]])

        fin_p[me, s] = own_p[z, me, s]
        for d in range(1, mpo):
            fp_copy(s, d).start()

    @pl.loop(0, sec_dev)
    def _(s):
        for d in range(1, mpo):
            fb_wait(s, d)
        total = fin_b[0, s].astype(F32)
        for m in range(1, mpo):
            total = total + fin_b[m, s].astype(F32)
        out_ref[s, mpo * hx:, :] = total.astype(BF16)
        for d in range(1, mpo):
            fp_wait(s, d)
        for m in range(mpo):
            out_ref[s, m * hx:(m + 1) * hx, :] = fin_p[m, s]

    @pl.loop(0, n)
    def _(t):
        if cores == 2:
            sib_copy(t).wait_send()

        @pl.loop(0, sec_dev)
        def _(s):
            for d in range(1, mpo):
                x_copy(t, s, d).wait_send()

            @pl.when(t != z)
            def _():
                zp_copy(t, s, t, right_dev).wait_send()
                zb_copy(t, s, t, right_dev).wait_send()

    @pl.loop(0, sec_dev)
    def _(s):
        for d in range(1, mpo):
            fp_copy(s, d).wait_send()
            fb_copy(s, d).wait_send()


def local(mesh, psi, left_env, right_env, targets):
    sec_count, mpo = mesh.shape["sec"], mesh.shape["mpo"]
    cores = 2 if mesh.shape["sub"] == 1 and sec_count % 2 == 0 else 1
    n = sec_count // cores
    sec_dev, width = psi.shape[:2]
    terms = left_env.shape[0] * sec_dev
    cols = right_env.shape[-1]
    cap = max(2, -(-terms // sec_count))
    hx = first_rows(width, mpo)
    hb = width - mpo * hx
    flat = targets.T.reshape(terms)
    owner, within = flat // sec_dev, flat % sec_dev
    rows = jnp.arange(terms)
    earlier = (owner[:, None] == owner[None, :]) & (rows[None, :] < rows[:, None])
    slot = owner * cap + jnp.sum(earlier.astype(jnp.int32), axis=1)
    placing = jnp.arange(sec_count * cap)[:, None] == slot[None, :]
    slots = jnp.sum(jnp.where(placing, rows[None, :], 0), axis=1).astype(jnp.int32)
    marks = jnp.any(
        placing[:, None, :] & (within[None, None, :] == jnp.arange(sec_dev)[None, :, None]), axis=2
    ).astype(F32).reshape(-1)

    vm = lambda *shape: pltpu.VMEM(shape, BF16)
    sem = lambda *shape: pltpu.SemaphoreType.DMA(shape)
    sib = (n, sec_dev, width, cols) if cores == 2 else (1, 1, 16, 128)
    xs = max(mpo - 1, 1)
    return pl.pallas_call(
        functools.partial(kernel, n, cores, mpo, cap, hx),
        out_shape=jax.ShapeDtypeStruct((sec_dev, width, cols), BF16),
        in_specs=[pl.BlockSpec(memory_space=pltpu.SMEM)] * 2 + [pl.BlockSpec(memory_space=pl.ANY)] * 3,
        out_specs=pl.BlockSpec(memory_space=pltpu.VMEM),
        scratch_shapes=[
            vm(sec_dev, width, width), vm(terms, width, width), vm(terms, width, cols),
            vm(*sib), vm(*sib),
            vm(n, mpo, sec_dev, hx, cols), vm(n, sec_dev, hb, cols),
            vm(xs, n, sec_dev, hx, cols),
            vm(n + 1, sec_dev, hx, cols), vm(n + 1, sec_dev, hb, cols),
            vm(mpo, sec_dev, hx, cols), vm(mpo, sec_dev, hb, cols),
            sem(2 * terms + 1), sem(n), sem(n),
            sem(xs, n, sec_dev), sem(xs, n, sec_dev),
            sem(n, sec_dev), sem(n + 1, sec_dev), sem(n, sec_dev), sem(n + 1, sec_dev),
            sem(xs, sec_dev), sem(mpo, sec_dev), sem(xs, sec_dev), sem(mpo, sec_dev),
        ],
        compiler_params=pltpu.CompilerParams(
            collective_id=0, has_side_effects=True, vmem_limit_bytes=60 * 1024 * 1024
        ),
        cost_estimate=pl.CostEstimate(
            flops=4 * terms * width * width * cols,
            bytes_accessed=2 * terms * width * (width + cols), transcendentals=0,
        ),
    )(
        slots, marks, psi, left_env.reshape(terms, width, width), right_env.reshape(terms, width, cols)
    )


def solution(mesh):
    placed = (
        P(("grp", "sec"), None, None),
        P("mpo", ("grp", "sec"), None, None),
        P("mpo", ("grp", "sec"), None, "sub"),
        P("sec", "mpo"),
    )
    return jax.shard_map(
        functools.partial(local, mesh), mesh=mesh, in_specs=placed,
        out_specs=P(("grp", "sec"), None, "sub"), check_vma=False,
    )
```

```python
import functools

import jax
import jax.numpy as jnp
from jax import lax
from jax.experimental import pallas as pl
from jax.experimental.pallas import tpu as pltpu
from jax.sharding import PartitionSpec as P

MESH = pl.DeviceIdType.MESH
F32 = jnp.float32
BF16 = jnp.bfloat16


def first_rows(width, mpo):
    return max(16, (width * 2 // 3 // mpo + 8) // 16 * 16)


def kernel(
    n, cores, mpo, cap, hx,
    targets_ref, psi_hbm, left_hbm, right_hbm, out_ref,
    slots_ref, marks_ref, pv, lv, rv, sib_send, sib_recv, own_p, own_b, x_recv, z_p, z_b, fin_p, fin_b,
    in_sem, sib_ssem, sib_rsem, x_ssem, x_rsem, zp_ssem, zp_rsem, zb_ssem, zb_rsem,
    fp_ssem, fp_rsem, fb_ssem, fb_rsem,
):
    terms = lv.shape[0]
    sec_dev, width, cols = pv.shape[0], lv.shape[1], rv.shape[2]
    hb = width - mpo * hx
    sec = lax.axis_index("sec")
    me = lax.axis_index("mpo")
    z = lax.div(sec, cores)
    c = lax.rem(sec, cores)
    sibling = {"sec": z * cores + (1 - c)}
    right_dev = {"sec": sec + cores}
    left_dev = {"sec": sec - cores}

    def other(d):
        return lax.rem(me + d, mpo)

    def load_psi():
        return pltpu.make_async_copy(psi_hbm, pv, in_sem.at[2 * terms])

    def load_right(r):
        return pltpu.make_async_copy(right_hbm.at[r], rv.at[r], in_sem.at[r])

    def load_left(r):
        return pltpu.make_async_copy(left_hbm.at[r], lv.at[r], in_sem.at[terms + r])

    load_psi().start()

    @pl.loop(0, terms)
    def _(r):
        load_right(r).start()

    @pl.loop(0, terms)
    def _(r):
        load_left(r).start()

    barrier = pltpu.get_barrier_semaphore()
    if cores == 2:
        pl.semaphore_signal(barrier, inc=1, device_id=sibling, device_id_type=MESH)
    for d in range(1, mpo):
        pl.semaphore_signal(barrier, inc=1, device_id={"mpo": other(d)}, device_id_type=MESH)

    @pl.when(z > 0)
    def _():
        pl.semaphore_signal(barrier, inc=1, device_id=left_dev, device_id_type=MESH)

    @pl.when(z < n - 1)
    def _():
        pl.semaphore_signal(barrier, inc=1, device_id=right_dev, device_id_type=MESH)

    goals = [targets_ref[r % sec_dev, r // sec_dev] for r in range(terms)]

    @pl.loop(0, n * cores)
    def _(owner):
        low = owner * sec_dev
        count = jnp.int32(0)
        row = [jnp.int32(0)] * cap
        goal = [jnp.int32(-1)] * cap
        for r in range(terms):
            hit = jnp.logical_and(goals[r] >= low, goals[r] < low + sec_dev)
            for i in range(cap):
                take = jnp.logical_and(hit, count == i)
                row[i] = jnp.where(take, r, row[i])
                goal[i] = jnp.where(take, goals[r], goal[i])
            count = count + jnp.where(hit, 1, 0)
        for i in range(cap):
            slots_ref[owner * cap + i] = row[i]
            for s in range(sec_dev):
                marks_ref[(owner * cap + i) * sec_dev + s] = jnp.where(goal[i] == low + s, 1.0, 0.0).astype(F32)

    peers = cores - 1 + mpo - 1 + jnp.minimum(z, 1) + jnp.minimum(n - 1 - z, 1)
    pl.semaphore_wait(barrier, peers)

    def target(k):
        near_left = 2 * z <= n - 1
        lead = jnp.where(near_left, n - 1 - 2 * z, 2 * z - (n - 1))
        q = jnp.maximum(k - lead, 0)
        half = lax.div(q, 2)
        odd = lax.rem(q, 2) == 1
        ahead = jnp.minimum(k, lead)
        t_left = jnp.where(odd, half, n - 1 - ahead - half)
        t_right = jnp.where(odd, n - 1 - half, ahead + half)
        return jnp.where(near_left, t_left, t_right)

    def sib_copy(t, row0, rows, i):
        return pltpu.make_async_remote_copy(
            src_ref=sib_send.at[t, :, row0:row0 + rows], dst_ref=sib_recv.at[t, :, row0:row0 + rows],
            send_sem=sib_ssem.at[t, i], recv_sem=sib_rsem.at[t, i],
            device_id=sibling, device_id_type=MESH)

    def x_copy(t, s, d):
        return pltpu.make_async_remote_copy(
            src_ref=own_p.at[t, other(d), s], dst_ref=x_recv.at[mpo - d - 1, t, s],
            send_sem=x_ssem.at[d - 1, t, s], recv_sem=x_rsem.at[mpo - d - 1, t, s],
            device_id={"mpo": other(d)}, device_id_type=MESH)

    def x_wait(t, s, d):
        pltpu.make_async_remote_copy(
            src_ref=own_p.at[t, other(d), s], dst_ref=x_recv.at[d - 1, t, s],
            send_sem=x_ssem.at[d - 1, t, s], recv_sem=x_rsem.at[d - 1, t, s],
            device_id={"mpo": other(d)}, device_id_type=MESH).wait_recv()

    def zp_copy(t, s, slot, dev):
        return pltpu.make_async_remote_copy(
            src_ref=own_p.at[t, me, s], dst_ref=z_p.at[slot, s],
            send_sem=zp_ssem.at[t, s], recv_sem=zp_rsem.at[slot, s],
            device_id=dev, device_id_type=MESH)

    def zb_copy(t, s, slot, dev):
        return pltpu.make_async_remote_copy(
            src_ref=own_b.at[t, s], dst_ref=z_b.at[slot, s],
            send_sem=zb_ssem.at[t, s], recv_sem=zb_rsem.at[slot, s],
            device_id=dev, device_id_type=MESH)

    def z_send(copy, t, s):
        @pl.when(t > z)
        def _():
            copy(t, s, t, right_dev).start()

        @pl.when(t < z)
        def _():
            copy(t, s, jnp.where(t == z - 1, n, t), left_dev).start()

    def fp_copy(s, d):
        return pltpu.make_async_remote_copy(
            src_ref=fin_p.at[me, s], dst_ref=fin_p.at[me, s],
            send_sem=fp_ssem.at[d - 1, s], recv_sem=fp_rsem.at[me, s],
            device_id={"mpo": other(d)}, device_id_type=MESH)

    def fb_copy(s, d):
        return pltpu.make_async_remote_copy(
            src_ref=fin_b.at[me, s], dst_ref=fin_b.at[me, s],
            send_sem=fb_ssem.at[d - 1, s], recv_sem=fb_rsem.at[me, s],
            device_id={"mpo": other(d)}, device_id_type=MESH)

    def fp_wait(s, d):
        o = other(d)
        pltpu.make_async_remote_copy(
            src_ref=fin_p.at[o, s], dst_ref=fin_p.at[o, s],
            send_sem=fp_ssem.at[d - 1, s], recv_sem=fp_rsem.at[o, s],
            device_id={"mpo": o}, device_id_type=MESH).wait_recv()

    def fb_wait(s, d):
        o = other(d)
        pltpu.make_async_remote_copy(
            src_ref=fin_b.at[o, s], dst_ref=fin_b.at[o, s],
            send_sem=fb_ssem.at[d - 1, s], recv_sem=fb_rsem.at[o, s],
            device_id={"mpo": o}, device_id_type=MESH).wait_recv()

    def add_to(ref, values):
        total = ref[...].astype(F32)
        for v in values:
            total = total + v.astype(F32)
        ref[...] = total.astype(BF16)

    load_psi().wait()
    @pl.loop(0, terms // sec_dev)
    def _(w):
        for j in range(sec_dev):
            load_right(w * sec_dev + j).wait()
        for j in range(sec_dev):
            r = w * sec_dev + j
            rv[r] = jnp.dot(pv[j], rv[r], preferred_element_type=F32).astype(BF16)

    @pl.loop(0, terms)
    def _(r):
        load_left(r).wait()

    def partial_rows(owner, row0, rows):
        products = []
        for i in range(cap):
            r = slots_ref[owner * cap + i]
            products.append(jnp.dot(lv[r, row0:row0 + rows, :], rv[r], preferred_element_type=F32))
        for s in range(sec_dev):
            total = None
            for i in range(cap):
                term = products[i] * marks_ref[(owner * cap + i) * sec_dev + s]
                total = term if total is None else total + term
            yield s, total.astype(BF16)

    parts = [(mpo * hx, hb, None)] + [(m * hx, hx, m) for m in range(mpo)]

    def make_sums(t):
        if cores == 2:
            for i, (row0, rows, m) in enumerate(parts):
                for s, value in partial_rows(t * cores + (1 - c), row0, rows):
                    sib_send[t, s, row0:row0 + rows, :] = value
                sib_copy(t, row0, rows, i).start()
        for row0, rows, m in parts:
            for s, value in partial_rows(t * cores + c, row0, rows):
                if m is None:
                    own_b[t, s] = value
                else:
                    own_p[t, m, s] = value

    def add_sibling(t):
        if cores == 2:
            for i, (row0, rows, m) in enumerate(parts):
                sib_copy(t, row0, rows, i).wait_recv()
                for s in range(sec_dev):
                    ref = own_b.at[t, s] if m is None else own_p.at[t, m, s]
                    add_to(ref, [sib_recv[t, s, row0:row0 + rows, :]])
                if m is None:
                    send_b(t)
        else:
            send_b(t)
        for s in range(sec_dev):
            for d in range(1, mpo):
                x_copy(t, s, d).start()

    def send_b(t):
        @pl.when(jnp.logical_and(z == 0, t > 0))
        def _():
            for s in range(sec_dev):
                zb_copy(t, s, t, right_dev).start()

        @pl.when(jnp.logical_and(z == n - 1, t < n - 1))
        def _():
            for s in range(sec_dev):
                zb_copy(t, s, jnp.where(t == z - 1, n, t), left_dev).start()

    @pl.loop(0, n)
    def _(k):
        make_sums(target(k))
        add_sibling(target(k))

    def pass_b(t, s, upstream):
        @pl.when(upstream)
        def _():
            zb_copy(t, s, t, right_dev).wait_recv()
            add_to(own_b.at[t, s], [z_b[t, s]])
            z_send(zb_copy, t, s)

    def pass_p(t, s, upstream):
        for d in range(1, mpo):
            x_wait(t, s, d)
        over_x = [x_recv[d, t, s] for d in range(mpo - 1)]

        @pl.when(upstream)
        def _():
            zp_copy(t, s, t, right_dev).wait_recv()
            add_to(own_p.at[t, me, s], over_x + [z_p[t, s]])

        @pl.when(jnp.logical_not(upstream))
        def _():
            add_to(own_p.at[t, me, s], over_x)

        z_send(zp_copy, t, s)

    def along_z(pass_on):
        @pl.loop(0, n - 1)
        def _(step):
            @pl.loop(0, sec_dev)
            def _(s):
                @pl.when(step >= z)
                def _():
                    pass_on(n - 1 - (step - z), s, z > 0)

                @pl.when(step >= n - 1 - z)
                def _():
                    pass_on(step - (n - 1 - z), s, z < n - 1)

    along_z(pass_b)

    @pl.loop(0, sec_dev)
    def _(s):
        @pl.when(z > 0)
        def _():
            zb_copy(z, s, z, left_dev).wait_recv()
            add_to(own_b.at[z, s], [z_b[z, s]])

        @pl.when(z < n - 1)
        def _():
            zb_copy(z, s, n, right_dev).wait_recv()
            add_to(own_b.at[z, s], [z_b[n, s]])

        fin_b[me, s] = own_b[z, s]
        for d in range(1, mpo):
            fb_copy(s, d).start()

    along_z(pass_p)

    @pl.loop(0, sec_dev)
    def _(s):
        for d in range(1, mpo):
            x_wait(z, s, d)
        add_to(own_p.at[z, me, s], [x_recv[d, z, s] for d in range(mpo - 1)])

        @pl.when(z > 0)
        def _():
            zp_copy(z, s, z, left_dev).wait_recv()
            add_to(own_p.at[z, me, s], [z_p[z, s]])

        @pl.when(z < n - 1)
        def _():
            zp_copy(z, s, n, right_dev).wait_recv()
            add_to(own_p.at[z, me, s], [z_p[n, s]])

        fin_p[me, s] = own_p[z, me, s]
        for d in range(1, mpo):
            fp_copy(s, d).start()

    @pl.loop(0, sec_dev)
    def _(s):
        for d in range(1, mpo):
            fb_wait(s, d)
        total = fin_b[0, s].astype(F32)
        for m in range(1, mpo):
            total = total + fin_b[m, s].astype(F32)
        out_ref[s, mpo * hx:, :] = total.astype(BF16)
        for d in range(1, mpo):
            fp_wait(s, d)
        for m in range(mpo):
            out_ref[s, m * hx:(m + 1) * hx, :] = fin_p[m, s]

    @pl.loop(0, n)
    def _(t):
        if cores == 2:
            for i, (row0, rows, m) in enumerate(parts):
                sib_copy(t, row0, rows, i).wait_send()

        @pl.loop(0, sec_dev)
        def _(s):
            for d in range(1, mpo):
                x_copy(t, s, d).wait_send()

            @pl.when(t != z)
            def _():
                zp_copy(t, s, t, right_dev).wait_send()
                zb_copy(t, s, t, right_dev).wait_send()

    @pl.loop(0, sec_dev)
    def _(s):
        for d in range(1, mpo):
            fp_copy(s, d).wait_send()
            fb_copy(s, d).wait_send()


def local(mesh, psi, left_env, right_env, targets):
    sec_count, mpo = mesh.shape["sec"], mesh.shape["mpo"]
    cores = 2 if mesh.shape["sub"] == 1 and sec_count % 2 == 0 else 1
    n = sec_count // cores
    sec_dev, width = psi.shape[:2]
    terms = left_env.shape[0] * sec_dev
    cols = right_env.shape[-1]
    cap = max(2, -(-terms // sec_count))
    hx = first_rows(width, mpo)
    hb = width - mpo * hx
    vm = lambda *shape: pltpu.VMEM(shape, BF16)
    sem = lambda *shape: pltpu.SemaphoreType.DMA(shape)
    sib = (n, sec_dev, width, cols) if cores == 2 else (1, 1, 16, 128)
    xs = max(mpo - 1, 1)
    return pl.pallas_call(
        functools.partial(kernel, n, cores, mpo, cap, hx),
        out_shape=jax.ShapeDtypeStruct((sec_dev, width, cols), BF16),
        in_specs=[pl.BlockSpec(memory_space=pltpu.SMEM)] + [pl.BlockSpec(memory_space=pl.ANY)] * 3,
        out_specs=pl.BlockSpec(memory_space=pltpu.VMEM),
        scratch_shapes=[
            pltpu.SMEM((sec_count * cap,), jnp.int32), pltpu.SMEM((sec_count * cap * sec_dev,), F32),
            vm(sec_dev, width, width), vm(terms, width, width), vm(terms, width, cols),
            vm(*sib), vm(*sib),
            vm(n, mpo, sec_dev, hx, cols), vm(n, sec_dev, hb, cols),
            vm(xs, n, sec_dev, hx, cols),
            vm(n + 1, sec_dev, hx, cols), vm(n + 1, sec_dev, hb, cols),
            vm(mpo, sec_dev, hx, cols), vm(mpo, sec_dev, hb, cols),
            sem(2 * terms + 1), sem(n, mpo + 1), sem(n, mpo + 1),
            sem(xs, n, sec_dev), sem(xs, n, sec_dev),
            sem(n, sec_dev), sem(n + 1, sec_dev), sem(n, sec_dev), sem(n + 1, sec_dev),
            sem(xs, sec_dev), sem(mpo, sec_dev), sem(xs, sec_dev), sem(mpo, sec_dev),
        ],
        compiler_params=pltpu.CompilerParams(
            collective_id=0, has_side_effects=True, vmem_limit_bytes=60 * 1024 * 1024
        ),
        cost_estimate=pl.CostEstimate(
            flops=4 * terms * width * width * cols,
            bytes_accessed=2 * terms * width * (width + cols), transcendentals=0,
        ),
    )(
        targets, psi, left_env.reshape(terms, width, width), right_env.reshape(terms, width, cols)
    )


def solution(mesh):
    placed = (
        P(("grp", "sec"), None, None),
        P("mpo", ("grp", "sec"), None, None),
        P("mpo", ("grp", "sec"), None, "sub"),
        P("sec", "mpo"),
    )
    return jax.shard_map(
        functools.partial(local, mesh), mesh=mesh, in_specs=placed,
        out_specs=P(("grp", "sec"), None, "sub"), check_vma=False,
    )
```

```python
import functools

import jax
import jax.numpy as jnp
from jax import lax
from jax.experimental import pallas as pl
from jax.experimental.pallas import tpu as pltpu
from jax.sharding import PartitionSpec as P

MESH = pl.DeviceIdType.MESH
F32 = jnp.float32
BF16 = jnp.bfloat16


def first_rows(width, mpo):
    return max(16, (width * 2 // 3 // mpo + 8) // 16 * 16)


def kernel(
    n, cores, mpo, cap, hx,
    targets_ref, psi_hbm, left_hbm, right_hbm, out_ref,
    slots_ref, marks_ref, pv, lv, rv, sib_send, sib_recv, own_p, own_b, x_recv, z_p, z_b, fin_p, fin_b,
    in_sem, sib_ssem, sib_rsem, x_ssem, x_rsem, zp_ssem, zp_rsem, zb_ssem, zb_rsem,
    fp_ssem, fp_rsem, fb_ssem, fb_rsem,
):
    terms = lv.shape[0]
    sec_dev, width, cols = pv.shape[0], lv.shape[1], rv.shape[2]
    hb = width - mpo * hx
    sec = lax.axis_index("sec")
    me = lax.axis_index("mpo")
    z = lax.div(sec, cores)
    c = lax.rem(sec, cores)
    sibling = {"sec": z * cores + (1 - c)}
    right_dev = {"sec": sec + cores}
    left_dev = {"sec": sec - cores}

    def other(d):
        return lax.rem(me + d, mpo)

    def load_psi():
        return pltpu.make_async_copy(psi_hbm, pv, in_sem.at[2 * terms])

    def load_right(r):
        return pltpu.make_async_copy(right_hbm.at[r], rv.at[r], in_sem.at[r])

    def load_left(r):
        return pltpu.make_async_copy(left_hbm.at[r], lv.at[r], in_sem.at[terms + r])

    barrier = pltpu.get_barrier_semaphore()
    if cores == 2:
        pl.semaphore_signal(barrier, inc=1, device_id=sibling, device_id_type=MESH)
    for d in range(1, mpo):
        pl.semaphore_signal(barrier, inc=1, device_id={"mpo": other(d)}, device_id_type=MESH)

    @pl.when(z > 0)
    def _():
        pl.semaphore_signal(barrier, inc=1, device_id=left_dev, device_id_type=MESH)

    @pl.when(z < n - 1)
    def _():
        pl.semaphore_signal(barrier, inc=1, device_id=right_dev, device_id_type=MESH)

    load_psi().start()

    @pl.loop(0, terms)
    def _(r):
        load_right(r).start()

    @pl.loop(0, terms)
    def _(r):
        load_left(r).start()

    goals = [targets_ref[r % sec_dev, r // sec_dev] for r in range(terms)]

    @pl.loop(0, n * cores)
    def _(owner):
        low = owner * sec_dev
        count = jnp.int32(0)
        row = [jnp.int32(0)] * cap
        goal = [jnp.int32(-1)] * cap
        for r in range(terms):
            hit = jnp.logical_and(goals[r] >= low, goals[r] < low + sec_dev)
            for i in range(cap):
                take = jnp.logical_and(hit, count == i)
                row[i] = jnp.where(take, r, row[i])
                goal[i] = jnp.where(take, goals[r], goal[i])
            count = count + jnp.where(hit, 1, 0)
        for i in range(cap):
            slots_ref[owner * cap + i] = row[i]
            for s in range(sec_dev):
                marks_ref[(owner * cap + i) * sec_dev + s] = jnp.where(goal[i] == low + s, 1.0, 0.0).astype(F32)

    peers = cores - 1 + mpo - 1 + jnp.minimum(z, 1) + jnp.minimum(n - 1 - z, 1)
    pl.semaphore_wait(barrier, peers)

    def target(k):
        near_left = 2 * z <= n - 1
        lead = jnp.where(near_left, n - 1 - 2 * z, 2 * z - (n - 1))
        q = jnp.maximum(k - lead, 0)
        half = lax.div(q, 2)
        odd = lax.rem(q, 2) == 1
        ahead = jnp.minimum(k, lead)
        t_left = jnp.where(odd, half, n - 1 - ahead - half)
        t_right = jnp.where(odd, n - 1 - half, ahead + half)
        return jnp.where(near_left, t_left, t_right)

    def sib_copy(t, row0, rows, i):
        return pltpu.make_async_remote_copy(
            src_ref=sib_send.at[t, :, row0:row0 + rows], dst_ref=sib_recv.at[t, :, row0:row0 + rows],
            send_sem=sib_ssem.at[t, i], recv_sem=sib_rsem.at[t, i],
            device_id=sibling, device_id_type=MESH)

    def x_copy(t, s, d):
        return pltpu.make_async_remote_copy(
            src_ref=own_p.at[t, other(d), s], dst_ref=x_recv.at[mpo - d - 1, t, s],
            send_sem=x_ssem.at[d - 1, t, s], recv_sem=x_rsem.at[mpo - d - 1, t, s],
            device_id={"mpo": other(d)}, device_id_type=MESH)

    def x_wait(t, s, d):
        pltpu.make_async_remote_copy(
            src_ref=own_p.at[t, other(d), s], dst_ref=x_recv.at[d - 1, t, s],
            send_sem=x_ssem.at[d - 1, t, s], recv_sem=x_rsem.at[d - 1, t, s],
            device_id={"mpo": other(d)}, device_id_type=MESH).wait_recv()

    def zp_copy(t, s, slot, dev):
        return pltpu.make_async_remote_copy(
            src_ref=own_p.at[t, me, s], dst_ref=z_p.at[slot, s],
            send_sem=zp_ssem.at[t, s], recv_sem=zp_rsem.at[slot, s],
            device_id=dev, device_id_type=MESH)

    def zb_copy(t, s, slot, dev):
        return pltpu.make_async_remote_copy(
            src_ref=own_b.at[t, s], dst_ref=z_b.at[slot, s],
            send_sem=zb_ssem.at[t, s], recv_sem=zb_rsem.at[slot, s],
            device_id=dev, device_id_type=MESH)

    def z_send(copy, t, s):
        @pl.when(t > z)
        def _():
            copy(t, s, t, right_dev).start()

        @pl.when(t < z)
        def _():
            copy(t, s, jnp.where(t == z - 1, n, t), left_dev).start()

    def fp_copy(s, d):
        return pltpu.make_async_remote_copy(
            src_ref=fin_p.at[me, s], dst_ref=fin_p.at[me, s],
            send_sem=fp_ssem.at[d - 1, s], recv_sem=fp_rsem.at[me, s],
            device_id={"mpo": other(d)}, device_id_type=MESH)

    def fb_copy(s, d):
        return pltpu.make_async_remote_copy(
            src_ref=fin_b.at[me, s], dst_ref=fin_b.at[me, s],
            send_sem=fb_ssem.at[d - 1, s], recv_sem=fb_rsem.at[me, s],
            device_id={"mpo": other(d)}, device_id_type=MESH)

    def fp_wait(s, d):
        o = other(d)
        pltpu.make_async_remote_copy(
            src_ref=fin_p.at[o, s], dst_ref=fin_p.at[o, s],
            send_sem=fp_ssem.at[d - 1, s], recv_sem=fp_rsem.at[o, s],
            device_id={"mpo": o}, device_id_type=MESH).wait_recv()

    def fb_wait(s, d):
        o = other(d)
        pltpu.make_async_remote_copy(
            src_ref=fin_b.at[o, s], dst_ref=fin_b.at[o, s],
            send_sem=fb_ssem.at[d - 1, s], recv_sem=fb_rsem.at[o, s],
            device_id={"mpo": o}, device_id_type=MESH).wait_recv()

    def add_to(ref, values):
        total = ref[...].astype(F32)
        for v in values:
            total = total + v.astype(F32)
        ref[...] = total.astype(BF16)

    load_psi().wait()
    @pl.loop(0, terms // sec_dev)
    def _(w):
        for j in range(sec_dev):
            load_right(w * sec_dev + j).wait()
        for j in range(sec_dev):
            r = w * sec_dev + j
            rv[r] = jnp.dot(pv[j], rv[r], preferred_element_type=F32).astype(BF16)

    @pl.loop(0, terms)
    def _(r):
        load_left(r).wait()

    def partial_rows(owner, row0, rows):
        products = []
        for i in range(cap):
            r = slots_ref[owner * cap + i]
            products.append(jnp.dot(lv[r, row0:row0 + rows, :], rv[r], preferred_element_type=F32))
        for s in range(sec_dev):
            total = None
            for i in range(cap):
                term = products[i] * marks_ref[(owner * cap + i) * sec_dev + s]
                total = term if total is None else total + term
            yield s, total.astype(BF16)

    parts = [(mpo * hx, hb, None)] + [(m * hx, hx, m) for m in range(mpo)]

    def make_sums(t):
        if cores == 2:
            for i, (row0, rows, m) in enumerate(parts):
                for s, value in partial_rows(t * cores + (1 - c), row0, rows):
                    sib_send[t, s, row0:row0 + rows, :] = value
                sib_copy(t, row0, rows, i).start()
        for row0, rows, m in parts:
            for s, value in partial_rows(t * cores + c, row0, rows):
                if m is None:
                    own_b[t, s] = value
                else:
                    own_p[t, m, s] = value

    def add_sibling(t):
        if cores == 2:
            for i, (row0, rows, m) in enumerate(parts):
                sib_copy(t, row0, rows, i).wait_recv()
                for s in range(sec_dev):
                    ref = own_b.at[t, s] if m is None else own_p.at[t, m, s]
                    add_to(ref, [sib_recv[t, s, row0:row0 + rows, :]])
                if m is None:
                    send_b(t)
        else:
            send_b(t)
        for s in range(sec_dev):
            for d in range(1, mpo):
                x_copy(t, s, d).start()

    def send_b(t):
        @pl.when(jnp.logical_and(z == 0, t > 0))
        def _():
            for s in range(sec_dev):
                zb_copy(t, s, t, right_dev).start()

        @pl.when(jnp.logical_and(z == n - 1, t < n - 1))
        def _():
            for s in range(sec_dev):
                zb_copy(t, s, jnp.where(t == z - 1, n, t), left_dev).start()

    @pl.loop(0, n)
    def _(k):
        make_sums(target(k))
        add_sibling(target(k))

    def pass_b(t, s, upstream):
        @pl.when(upstream)
        def _():
            zb_copy(t, s, t, right_dev).wait_recv()
            add_to(own_b.at[t, s], [z_b[t, s]])
            z_send(zb_copy, t, s)

    def pass_p(t, s, upstream):
        for d in range(1, mpo):
            x_wait(t, s, d)
        over_x = [x_recv[d, t, s] for d in range(mpo - 1)]

        @pl.when(upstream)
        def _():
            zp_copy(t, s, t, right_dev).wait_recv()
            add_to(own_p.at[t, me, s], over_x + [z_p[t, s]])

        @pl.when(jnp.logical_not(upstream))
        def _():
            add_to(own_p.at[t, me, s], over_x)

        z_send(zp_copy, t, s)

    def along_z(pass_on, between):
        @pl.loop(0, n - 1)
        def _(step):
            if between is not None:
                pl.when(step == min(1, n - 2))(between)

            @pl.loop(0, sec_dev)
            def _(s):
                @pl.when(step >= z)
                def _():
                    pass_on(n - 1 - (step - z), s, z > 0)

                @pl.when(step >= n - 1 - z)
                def _():
                    pass_on(step - (n - 1 - z), s, z < n - 1)

    def own_rows_b():
        @pl.loop(0, sec_dev)
        def _(s):
            @pl.when(z > 0)
            def _():
                zb_copy(z, s, z, left_dev).wait_recv()
                add_to(own_b.at[z, s], [z_b[z, s]])

            @pl.when(z < n - 1)
            def _():
                zb_copy(z, s, n, right_dev).wait_recv()
                add_to(own_b.at[z, s], [z_b[n, s]])

            fin_b[me, s] = own_b[z, s]
            for d in range(1, mpo):
                fb_copy(s, d).start()

    along_z(pass_b, None)
    along_z(pass_p, own_rows_b)

    @pl.loop(0, sec_dev)
    def _(s):
        for d in range(1, mpo):
            x_wait(z, s, d)
        add_to(own_p.at[z, me, s], [x_recv[d, z, s] for d in range(mpo - 1)])

        @pl.when(z > 0)
        def _():
            zp_copy(z, s, z, left_dev).wait_recv()
            add_to(own_p.at[z, me, s], [z_p[z, s]])

        @pl.when(z < n - 1)
        def _():
            zp_copy(z, s, n, right_dev).wait_recv()
            add_to(own_p.at[z, me, s], [z_p[n, s]])

        fin_p[me, s] = own_p[z, me, s]
        for d in range(1, mpo):
            fp_copy(s, d).start()

    @pl.loop(0, sec_dev)
    def _(s):
        for d in range(1, mpo):
            fb_wait(s, d)
        total = fin_b[0, s].astype(F32)
        for m in range(1, mpo):
            total = total + fin_b[m, s].astype(F32)
        out_ref[s, mpo * hx:, :] = total.astype(BF16)
        for d in range(1, mpo):
            fp_wait(s, d)
        for m in range(mpo):
            out_ref[s, m * hx:(m + 1) * hx, :] = fin_p[m, s]

    @pl.loop(0, n)
    def _(t):
        if cores == 2:
            for i, (row0, rows, m) in enumerate(parts):
                sib_copy(t, row0, rows, i).wait_send()

        @pl.loop(0, sec_dev)
        def _(s):
            for d in range(1, mpo):
                x_copy(t, s, d).wait_send()

            @pl.when(t != z)
            def _():
                zp_copy(t, s, t, right_dev).wait_send()
                zb_copy(t, s, t, right_dev).wait_send()

    @pl.loop(0, sec_dev)
    def _(s):
        for d in range(1, mpo):
            fp_copy(s, d).wait_send()
            fb_copy(s, d).wait_send()


def local(mesh, psi, left_env, right_env, targets):
    sec_count, mpo = mesh.shape["sec"], mesh.shape["mpo"]
    cores = 2 if mesh.shape["sub"] == 1 and sec_count % 2 == 0 else 1
    n = sec_count // cores
    sec_dev, width = psi.shape[:2]
    terms = left_env.shape[0] * sec_dev
    cols = right_env.shape[-1]
    cap = max(2, -(-terms // sec_count))
    hx = first_rows(width, mpo)
    hb = width - mpo * hx
    vm = lambda *shape: pltpu.VMEM(shape, BF16)
    sem = lambda *shape: pltpu.SemaphoreType.DMA(shape)
    sib = (n, sec_dev, width, cols) if cores == 2 else (1, 1, 16, 128)
    xs = max(mpo - 1, 1)
    return pl.pallas_call(
        functools.partial(kernel, n, cores, mpo, cap, hx),
        out_shape=jax.ShapeDtypeStruct((sec_dev, width, cols), BF16),
        in_specs=[pl.BlockSpec(memory_space=pltpu.SMEM)] + [pl.BlockSpec(memory_space=pl.ANY)] * 3,
        out_specs=pl.BlockSpec(memory_space=pltpu.VMEM),
        scratch_shapes=[
            pltpu.SMEM((sec_count * cap,), jnp.int32), pltpu.SMEM((sec_count * cap * sec_dev,), F32),
            vm(sec_dev, width, width), vm(terms, width, width), vm(terms, width, cols),
            vm(*sib), vm(*sib),
            vm(n, mpo, sec_dev, hx, cols), vm(n, sec_dev, hb, cols),
            vm(xs, n, sec_dev, hx, cols),
            vm(n + 1, sec_dev, hx, cols), vm(n + 1, sec_dev, hb, cols),
            vm(mpo, sec_dev, hx, cols), vm(mpo, sec_dev, hb, cols),
            sem(2 * terms + 1), sem(n, mpo + 1), sem(n, mpo + 1),
            sem(xs, n, sec_dev), sem(xs, n, sec_dev),
            sem(n, sec_dev), sem(n + 1, sec_dev), sem(n, sec_dev), sem(n + 1, sec_dev),
            sem(xs, sec_dev), sem(mpo, sec_dev), sem(xs, sec_dev), sem(mpo, sec_dev),
        ],
        compiler_params=pltpu.CompilerParams(
            collective_id=0, has_side_effects=True, vmem_limit_bytes=60 * 1024 * 1024
        ),
        cost_estimate=pl.CostEstimate(
            flops=4 * terms * width * width * cols,
            bytes_accessed=2 * terms * width * (width + cols), transcendentals=0,
        ),
    )(
        targets, psi, left_env.reshape(terms, width, width), right_env.reshape(terms, width, cols)
    )


def solution(mesh):
    placed = (
        P(("grp", "sec"), None, None),
        P("mpo", ("grp", "sec"), None, None),
        P("mpo", ("grp", "sec"), None, "sub"),
        P("sec", "mpo"),
    )
    return jax.shard_map(
        functools.partial(local, mesh), mesh=mesh, in_specs=placed,
        out_specs=P(("grp", "sec"), None, "sub"), check_vma=False,
    )
```
